512 devices in a mesh: vid: 32 (over y, z_lo, core), aud: 16 (over z_hi, x).
Axes of the slice: x: 4, y: 4, z: 16 (z_hi: 4, z_lo: 4; z = z_hi * 4 + z_lo), core: 2. Of those that a mesh axis runs over, the one named last changes fastest.
Arguments:
- video_match: bfloat16 [8192, 1024], P(('vid', 'aud')), may hold values from -6 to 6
- video_value: bfloat16 [8192, 1024], P(('vid', 'aud')), may hold values from -6 to 6
- audio_match: bfloat16 [8192, 1024], P(('vid', 'aud')), may hold values from -6 to 6
- audio_value: bfloat16 [8192, 1024], P(('vid', 'aud')), may hold values from -6 to 6
- video_proj: bfloat16 [1024, 1024], replicated, may hold values from -0.1875 to 0.1875
- audio_proj: bfloat16 [1024, 1024], replicated, may hold values from -0.1875 to 0.1875
Outputs:
- video_out: bfloat16 [8192, 1024], P(('vid', 'aud'))
- audio_out: bfloat16 [8192, 1024], P(('vid', 'aud'))
The draws below stay inside these ranges and needn't reach their ends.
All inputs are finite; a program needn't handle non-finite values.
Results may differ from the reference program's by a relative error of at most 0.013.
Values may be sent and summed in bfloat16 or wider, within the bound.
A program may use at most 64 MiB of HBM per device.

```python
import math
import jax
import jax.numpy as jnp
from jax import lax

D = 1024
HEADS = 8
HEAD_DIM = 128
INNER = 1024
NV = 8192
NA = 8192


def draw_video_match(key, part):
    key = jax.random.fold_in(key, 5)
    return jnp.clip(1.4 * jax.random.normal(key, (NV, HEADS * HEAD_DIM), jnp.float32), -6.0, 6.0).astype(jnp.bfloat16)


def draw_audio_match(key, part):
    key = jax.random.fold_in(key, 9)
    return jnp.clip(1.4 * jax.random.normal(key, (NA, HEADS * HEAD_DIM), jnp.float32), -6.0, 6.0).astype(jnp.bfloat16)


def level_of(rng, dims, cuts, least, largest):
    def one(dim, shards_of):
        steps = jax.random.uniform(jax.random.fold_in(jax.random.fold_in(rng, 6), dim), (shards_of,), jnp.float32, least / len(cuts), largest / len(cuts))
        return jnp.repeat(jnp.exp(steps), dims[dim] // shards_of).reshape((-1,) + (1,) * (len(dims) - dim - 1))

    gain = one(*cuts[0])
    for cut in cuts[1:]:
        gain = gain * one(*cut)
    return gain


def centred(key, dims, spread, bound, shards=(), held_as=jnp.bfloat16):
    result = spread * jax.random.normal(key, dims, jnp.float32)
    if shards:
        result = result * level_of(key, dims, shards, -0.22, 0.18)
    return jnp.clip(result, -bound, bound).astype(held_as)


def setup_inputs(seed: int = 0) -> dict:
    arg_keys = jax.random.split(jax.random.key(seed), 7)
    return {
        "video_match": draw_video_match(jax.random.fold_in(arg_keys[6], 71), 0),
        "video_value": centred(arg_keys[1], (NV, INNER), 1.0, 6.0, ((0, 512),)),
        "audio_match": draw_audio_match(jax.random.fold_in(arg_keys[6], 71), 0),
        "audio_value": centred(arg_keys[3], (NA, INNER), 1.0, 6.0, ((0, 512),)),
        "video_proj": centred(arg_keys[4], (INNER, D), INNER ** -0.5, 0.1875),
        "audio_proj": centred(arg_keys[5], (INNER, D), INNER ** -0.5, 0.1875),
    }


def head_cols(field, head):
    return field[:, head * HEAD_DIM:(head + 1) * HEAD_DIM]


def tile_scores(block, keys, head):
    return jnp.dot(head_cols(block, head), head_cols(keys, head).T, preferred_element_type=jnp.float32) * (HEAD_DIM ** -0.5)


def reference(video_match, video_value, audio_match, audio_value, video_proj, audio_proj):
    step_rows = math.gcd(NV, 1024)
    blocks = NV // step_rows
    match_blocks = video_match.reshape(blocks, step_rows, HEADS * HEAD_DIM)
    value_blocks = video_value.reshape(blocks, step_rows, HEADS * HEAD_DIM)

    def peaks(carry, block):
        found = []
        for head in range(HEADS):
            score = tile_scores(block, audio_match, head)
            found.append(jnp.maximum(carry[head], score.max(0)))
        return jnp.stack(found), None

    col_top, _ = lax.scan(peaks, jnp.full((HEADS, NA), -jnp.inf, jnp.float32), match_blocks)

    def accumulate(carry, pair):
        col_sum, col_num = carry
        block, values = pair
        mixes, sums, nums = [], [], []
        for head in range(HEADS):
            score = tile_scores(block, audio_match, head)
            row_exp = jnp.exp(score - score.max(1, keepdims=True))
            row_num = jnp.dot(row_exp.astype(jnp.bfloat16), head_cols(audio_value, head), preferred_element_type=jnp.float32)
            mixes.append(row_num / row_exp.sum(1, keepdims=True))
            col_exp = jnp.exp(score - col_top[head][None, :])
            sums.append(col_sum[head] + col_exp.sum(0))
            nums.append(col_num[head] + lax.dot_general(col_exp.astype(jnp.bfloat16), head_cols(values, head), (((0,), (0,)), ((), ())), preferred_element_type=jnp.float32))
        return (jnp.stack(sums), jnp.stack(nums)), jnp.concatenate(mixes, 1).astype(jnp.bfloat16)

    start = (jnp.zeros((HEADS, NA), jnp.float32), jnp.zeros((HEADS, NA, HEAD_DIM), jnp.float32))
    (col_sum, col_num), video_mix = lax.scan(accumulate, start, (match_blocks, value_blocks))
    video_mix = video_mix.reshape(NV, HEADS * HEAD_DIM)
    video_out = jnp.dot(video_mix, video_proj, preferred_element_type=jnp.float32).astype(jnp.bfloat16)
    audio_mix = (col_num / col_sum[:, :, None]).transpose(1, 0, 2).reshape(NA, HEADS * HEAD_DIM).astype(jnp.bfloat16)
    audio_out = jnp.dot(audio_mix, audio_proj, preferred_element_type=jnp.float32).astype(jnp.bfloat16)
    return video_out, audio_out
```

```python
import math

import jax
import jax.numpy as jnp
from jax import lax
from jax.experimental import pallas as pl
from jax.experimental.pallas import tpu as pltpu
from jax.sharding import PartitionSpec as P

MESH = pl.DeviceIdType.MESH
HEADS = 8
DIM = 128
ROWS = 16
BLOCK = HEADS * ROWS
TOKENS = 8 * BLOCK
WIDTH = HEADS * DIM
STAT = BLOCK + 16
CHUNK = 256
SCALE = DIM ** (-0.5) * math.log2(math.e)
F32, BF16 = jnp.float32, jnp.bfloat16
NT = (((1,), (1,)), ((), ()))


def position():
    v, a = lax.axis_index("vid"), lax.axis_index("aud")
    return a % 4, v // 8, (a // 4) * 4 + (v // 2) % 4, v % 2


def device(place):
    x, y, z, c = place
    return ((y * 4 + z % 4) * 2 + c, (z // 4) * 4 + x)


def head_peer(place, k):
    x, y, z, c = place
    return x, y, (z + 2 * k + 16) % 16, c


def video_peer(place, k):
    x, y, z, c = place
    step = k // 2 if k >= 0 else -((-k) // 2)
    return (x + step + 4) % 4, y, z, (c + k) % 2 if k >= 0 else (c - k) % 2


def audio_peer(place, k):
    x, y, z, c = place
    step = k // 2 if k >= 0 else -((-k) // 2)
    return x, (y + step + 4) % 4, (z // 2) * 2 + (z + abs(k)) % 2, c


def send(src, dst, sems, n, place):
    return pltpu.make_async_remote_copy(
        src_ref=src,
        dst_ref=dst,
        send_sem=sems.at[0, n],
        recv_sem=sems.at[1, n],
        device_id=device(place),
        device_id_type=MESH,
    )


def attend(side, tile, values_t, out):
    keys = tile[:, 2 - 2 * side].reshape(TOKENS, DIM)

    def chunk(i, carry):
        slots = CHUNK // BLOCK
        queries = tile[pl.ds(i * slots, slots), 2 * side].reshape(CHUNK, DIM)
        score = lax.dot_general(keys, queries, NT, preferred_element_type=F32)
        peak = score.max(0, keepdims=True).astype(BF16).astype(F32)
        weight = jnp.exp2((score - peak) * SCALE)
        total = weight.sum(0, keepdims=True)
        num = jnp.dot(values_t[...], weight.astype(BF16), preferred_element_type=F32)
        high = total.astype(BF16).astype(F32)
        row = lax.broadcasted_iota(jnp.int32, (16, CHUNK), 0)
        stat = jnp.where(row == 0, peak, jnp.where(row == 1, high, jnp.where(row == 2, total - high, 0.0)))
        for s in range(slots):
            lanes = slice(s * BLOCK, (s + 1) * BLOCK)
            out[side, i * slots + s, :BLOCK] = num[:, lanes].astype(BF16)
            out[side, i * slots + s, BLOCK:] = stat[:, lanes].astype(BF16)
        return carry

    lax.fori_loop(0, TOKENS // CHUNK, chunk, 0)


def combine(side, part, back, mixed):
    def source(k):
        return part if k == 0 else back

    stats = [source(k)[side, k, BLOCK:].astype(F32) for k in range(8)]
    peaks = [s[0:1] for s in stats]
    top = peaks[0]
    for p in peaks[1:]:
        top = jnp.maximum(top, p)
    num = jnp.zeros((DIM, BLOCK), F32)
    total = jnp.zeros((1, BLOCK), F32)
    for k in range(8):
        gain = jnp.exp2((peaks[k] - top) * SCALE)
        total = total + gain * (stats[k][1:2] + stats[k][2:3])
        num = num + gain * source(k)[side, k, :BLOCK].astype(F32)
    mix = (num / total).T.astype(BF16)
    mixed[:, side] = mix.reshape(HEADS, ROWS, DIM)


def kernel(vm, vv, am, av, vproj, aproj, vout, aout,
           staged, tile, values_t, part, back, mixed, whole, weights,
           head_sems, gather_sems, return_sems, final_sems, local_sems):
    place = position()
    head = place[2] // 2

    loads = [
        pltpu.make_async_copy(vproj, weights.at[0], local_sems.at[0]),
        pltpu.make_async_copy(aproj, weights.at[1], local_sems.at[1]),
    ]
    for load in loads:
        load.start()

    barrier = pltpu.get_barrier_semaphore()
    for peer in (head_peer, video_peer, audio_peer):
        for k in range(1, 8):
            pl.semaphore_signal(barrier, inc=1, device_id=device(peer(place, k)), device_id_type=MESH)
    for n, array in enumerate((vm, vv, am, av)):
        for h in range(HEADS):
            staged[h, n] = array[:, h * DIM : (h + 1) * DIM]
    tile[0, :, :ROWS] = staged[head]
    pl.semaphore_wait(barrier, 21)

    sends = []
    for k in range(1, 8):
        peer = head_peer(place, k)
        sends.append(send(staged.at[peer[2] // 2], tile.at[0, :, pl.ds(k * ROWS, ROWS)], head_sems, k, peer))
    for s in sends:
        s.start()
    for s in sends:
        s.wait_recv()

    gathers = []
    for k in range(1, 8):
        gathers.append(send(tile.at[0, pl.ds(0, 2)], tile.at[k, pl.ds(0, 2)], gather_sems, k, video_peer(place, k)))
        gathers.append(send(tile.at[0, pl.ds(2, 2)], tile.at[k, pl.ds(2, 2)], gather_sems, 8 + k, audio_peer(place, k)))
    for s in gathers:
        s.start()
    for s in gathers:
        s.wait_recv()

    returns = []
    for side, peer in ((0, video_peer), (1, audio_peer)):
        for k in range(8):
            values_t[:, k * BLOCK : (k + 1) * BLOCK] = tile[k, 3 - 2 * side].T
        attend(side, tile, values_t, part)
        for k in range(1, 8):
            returns.append(send(part.at[side, k], back.at[side, k], return_sems, 8 * side + k, peer(place, -k)))
            returns[-1].start()
    for side in range(2):
        for s in returns[7 * side : 7 * side + 7]:
            s.wait_recv()
        combine(side, part, back, mixed)

    finals = []
    for k in range(1, 8):
        finals.append(send(mixed.at[k], whole.at[head], final_sems, k, head_peer(place, -k)))
        finals[-1].start()
    whole[head] = mixed[0]
    for load in loads:
        load.wait()
    for k, s in enumerate(finals):
        s.wait_recv()
    for side, out in ((0, vout), (1, aout)):
        mix = jnp.concatenate([whole[h, side] for h in range(HEADS)], axis=1)
        out[...] = jnp.dot(mix, weights[side], preferred_element_type=F32).astype(BF16)
    for s in sends + gathers + returns + finals:
        s.wait_send()


def shards(*args):
    vmem = pl.BlockSpec(memory_space=pltpu.VMEM)
    hbm = pl.BlockSpec(memory_space=pl.ANY)
    return pl.pallas_call(
        kernel,
        out_shape=[jax.ShapeDtypeStruct((ROWS, WIDTH), BF16)] * 2,
        in_specs=[vmem] * 4 + [hbm] * 2,
        out_specs=[vmem] * 2,
        scratch_shapes=[
            pltpu.VMEM((HEADS, 4, ROWS, DIM), BF16),
            pltpu.VMEM((8, 4, BLOCK, DIM), BF16),
            pltpu.VMEM((DIM, TOKENS), BF16),
            pltpu.VMEM((2, 8, STAT, DIM), BF16),
            pltpu.VMEM((2, 8, STAT, DIM), BF16),
            pltpu.VMEM((HEADS, 2, ROWS, DIM), BF16),
            pltpu.VMEM((HEADS, 2, ROWS, DIM), BF16),
            pltpu.VMEM((2, WIDTH, WIDTH), BF16),
            pltpu.SemaphoreType.DMA((2, 8)),
            pltpu.SemaphoreType.DMA((2, 16)),
            pltpu.SemaphoreType.DMA((2, 16)),
            pltpu.SemaphoreType.DMA((2, 8)),
            pltpu.SemaphoreType.DMA((2,)),
        ],
        compiler_params=pltpu.CompilerParams(
            collective_id=0, has_side_effects=True, vmem_limit_bytes=40 * 2**20
        ),
    )(*args)


def solution(mesh):
    tokens = P(("vid", "aud"), None)
    return jax.shard_map(
        shards,
        mesh=mesh,
        in_specs=(tokens,) * 4 + (P(), P()),
        out_specs=(tokens, tokens),
        check_vma=False,
    )
```

```python
import math

import jax
import jax.numpy as jnp
from jax import lax
from jax.experimental import pallas as pl
from jax.experimental.pallas import tpu as pltpu
from jax.sharding import PartitionSpec as P

MESH = pl.DeviceIdType.MESH
HEADS = 8
DIM = 128
ROWS = 16
BLOCK = HEADS * ROWS
TOKENS = 8 * BLOCK
WIDTH = HEADS * DIM
STAT = BLOCK + 16
PAIR = 2
CHUNK = PAIR * BLOCK
ORDER = (0, 1, 7, 2, 6, 3, 5, 4)
PARTS = ((0, 5), (5, 8))
SCALE = DIM ** (-0.5) * math.log2(math.e)
F32, BF16 = jnp.float32, jnp.bfloat16
NT = (((1,), (1,)), ((), ()))


def position():
    v, a = lax.axis_index("vid"), lax.axis_index("aud")
    return a % 4, v // 8, (a // 4) * 4 + (v // 2) % 4, v % 2


def device(place):
    x, y, z, c = place
    return ((y * 4 + z % 4) * 2 + c, (z // 4) * 4 + x)


def head_peer(place, k):
    x, y, z, c = place
    return x, y, (z + 2 * k + 16) % 16, c


def video_peer(place, k):
    x, y, z, c = place
    step = k // 2 if k >= 0 else -((-k) // 2)
    return (x + step + 4) % 4, y, z, (c + k) % 2 if k >= 0 else (c - k) % 2


def audio_peer(place, k):
    x, y, z, c = place
    step = k // 2 if k >= 0 else -((-k) // 2)
    return x, (y + step + 4) % 4, (z // 2) * 2 + (z + abs(k)) % 2, c


def send(src, dst, sems, n, place):
    return pltpu.make_async_remote_copy(
        src_ref=src,
        dst_ref=dst,
        send_sem=sems.at[0, n],
        recv_sem=sems.at[1, n],
        device_id=device(place),
        device_id_type=MESH,
    )


def attend(side, slot, tile, values_t, out):
    keys = tile[:, 2 - 2 * side].reshape(TOKENS, DIM)
    queries = tile[slot : slot + PAIR, 2 * side].reshape(CHUNK, DIM)
    score = lax.dot_general(keys, queries, NT, preferred_element_type=F32)
    peak = score.max(0, keepdims=True).astype(BF16).astype(F32)
    weight = jnp.exp2((score - peak) * SCALE)
    total = weight.sum(0, keepdims=True)
    num = jnp.dot(values_t[...], weight.astype(BF16), preferred_element_type=F32)
    high = total.astype(BF16).astype(F32)
    row = lax.broadcasted_iota(jnp.int32, (16, CHUNK), 0)
    stat = jnp.where(row == 0, peak, jnp.where(row == 1, high, jnp.where(row == 2, total - high, 0.0)))
    for s in range(PAIR):
        lanes = slice(s * BLOCK, (s + 1) * BLOCK)
        out[side, slot + s, :BLOCK] = num[:, lanes].astype(BF16)
        out[side, slot + s, BLOCK:] = stat[:, lanes].astype(BF16)


def combine(side, part, back, mixed):
    def source(k):
        return part if k == 0 else back

    stats = [source(k)[side, k, BLOCK:].astype(F32) for k in range(8)]
    peaks = [s[0:1] for s in stats]
    top = peaks[0]
    for p in peaks[1:]:
        top = jnp.maximum(top, p)
    num = jnp.zeros((DIM, BLOCK), F32)
    total = jnp.zeros((1, BLOCK), F32)
    for k in range(8):
        gain = jnp.exp2((peaks[k] - top) * SCALE)
        total = total + gain * (stats[k][1:2] + stats[k][2:3])
        num = num + gain * source(k)[side, k, :BLOCK].astype(F32)
    mix = (num / total).T.astype(BF16)
    mixed[side] = mix.reshape(HEADS, ROWS, DIM)


def kernel(vm, vv, am, av, vproj, aproj, vout, aout,
           tokens, staged, tile, values_t, part, back, mixed, whole, weights,
           head_sems, gather_sems, return_sems, final_sems, local_sems):
    place = position()
    head = place[2] // 2

    loads = [
        pltpu.make_async_copy(array, tokens.at[n], local_sems.at[n]) for n, array in enumerate((vm, vv, am, av))
    ] + [
        pltpu.make_async_copy(array, weights.at[n], local_sems.at[4 + n]) for n, array in enumerate((vproj, aproj))
    ]
    for load in loads:
        load.start()

    barrier = pltpu.get_barrier_semaphore()
    for peer in (head_peer, video_peer, audio_peer):
        for k in range(1, 8):
            pl.semaphore_signal(barrier, inc=1, device_id=device(peer(place, k)), device_id_type=MESH)
    for n in range(4):
        loads[n].wait()
        for h in range(HEADS):
            staged[h, n] = tokens[n, :, h * DIM : (h + 1) * DIM]
    tile[0, :, :ROWS] = staged[head]
    pl.semaphore_wait(barrier, 21)

    sends = {}
    for k in (4, 3, 5, 2, 6, 1, 7):
        peer = head_peer(place, k)
        rows = pl.ds(ORDER.index(k) * ROWS, ROWS)
        sends[k] = send(staged.at[peer[2] // 2], tile.at[0, :, rows], head_sems, k, peer)
        sends[k].start()

    gathers = []
    for n, (first, last) in enumerate(PARTS):
        for k in ORDER[first:last]:
            if k:
                sends[k].wait_recv()
        rows = pl.ds(first * ROWS, (last - first) * ROWS)
        for k in (4, 5, 2, 3, 6, 7, 1):
            for side, peer in ((0, video_peer), (1, audio_peer)):
                arrays = pl.ds(2 * side, 2)
                gathers.append(
                    send(tile.at[0, arrays, rows], tile.at[k, arrays, rows], gather_sems, 16 * n + 8 * side + k, peer(place, k))
                )
                gathers[-1].start()
    for s in gathers:
        s.wait_recv()

    returns = [[], []]
    for side, peer in ((0, video_peer), (1, audio_peer)):
        for k in range(8):
            values_t[:, k * BLOCK : (k + 1) * BLOCK] = tile[k, 3 - 2 * side].T
        for slot in range(8 - PAIR, -1, -PAIR):
            attend(side, slot, tile, values_t, part)
            for k in range(slot, slot + PAIR):
                if k:
                    returns[side].append(
                        send(part.at[side, k], back.at[side, k], return_sems, 8 * side + k, peer(place, -k))
                    )
                    returns[side][-1].start()

    finals = [[], []]
    for side in range(2):
        for s in returns[side]:
            s.wait_recv()
        combine(side, part, back, mixed)
        for k in (4, 3, 5, 2, 6, 1, 7):
            peer = head_peer(place, -k)
            finals[side].append(
                send(mixed.at[side, ORDER.index(k)], whole.at[side, head], final_sems, 8 * side + k, peer)
            )
            finals[side][-1].start()
        whole[side, head] = mixed[side, 0]
    for load in loads[4:]:
        load.wait()
    for side, out in ((0, vout), (1, aout)):
        for s in finals[side]:
            s.wait_recv()
        mix = jnp.concatenate([whole[side, h] for h in range(HEADS)], axis=1)
        out[...] = jnp.dot(mix, weights[side], preferred_element_type=F32).astype(BF16)
    for s in [*sends.values(), *gathers, *returns[0], *returns[1], *finals[0], *finals[1]]:
        s.wait_send()


def shards(*args):
    vmem = pl.BlockSpec(memory_space=pltpu.VMEM)
    hbm = pl.BlockSpec(memory_space=pl.ANY)
    return pl.pallas_call(
        kernel,
        out_shape=[jax.ShapeDtypeStruct((ROWS, WIDTH), BF16)] * 2,
        in_specs=[hbm] * 6,
        out_specs=[vmem] * 2,
        scratch_shapes=[
            pltpu.VMEM((4, ROWS, WIDTH), BF16),
            pltpu.VMEM((HEADS, 4, ROWS, DIM), BF16),
            pltpu.VMEM((8, 4, BLOCK, DIM), BF16),
            pltpu.VMEM((DIM, TOKENS), BF16),
            pltpu.VMEM((2, 8, STAT, DIM), BF16),
            pltpu.VMEM((2, 8, STAT, DIM), BF16),
            pltpu.VMEM((2, HEADS, ROWS, DIM), BF16),
            pltpu.VMEM((2, HEADS, ROWS, DIM), BF16),
            pltpu.VMEM((2, WIDTH, WIDTH), BF16),
            pltpu.SemaphoreType.DMA((2, 8)),
            pltpu.SemaphoreType.DMA((2, 16 * len(PARTS))),
            pltpu.SemaphoreType.DMA((2, 16)),
            pltpu.SemaphoreType.DMA((2, 16)),
            pltpu.SemaphoreType.DMA((6,)),
        ],
        compiler_params=pltpu.CompilerParams(
            collective_id=0, has_side_effects=True, vmem_limit_bytes=60 * 2**20
        ),
    )(*args)


def solution(mesh):
    tokens = P(("vid", "aud"), None)
    return jax.shard_map(
        shards,
        mesh=mesh,
        in_specs=(tokens,) * 4 + (P(), P()),
        out_specs=(tokens, tokens),
        check_vma=False,
    )
```

```python
import math

import jax
import jax.numpy as jnp
from jax import lax
from jax.experimental import pallas as pl
from jax.experimental.pallas import tpu as pltpu
from jax.sharding import PartitionSpec as P

MESH = pl.DeviceIdType.MESH
HEADS = 8
DIM = 128
ROWS = 16
BLOCK = HEADS * ROWS
TOKENS = 8 * BLOCK
WIDTH = HEADS * DIM
STAT = BLOCK + 16
KERNEL_VMEM = 32 * 2**20
FIRST = (4, 1, 7, 2, 6, 3, 5)
WIDE = 4
STEP = 2
ORDER = (0, 1, 7, 2, 6, 3, 5, 4)
PARTS = ((0, 0, 5), (0, 5, 8), (1, 0, 5), (1, 5, 8))
SCALE = DIM ** (-0.5) * math.log2(math.e)
F32, BF16 = jnp.float32, jnp.bfloat16
NT = (((1,), (1,)), ((), ()))


def position():
    v, a = lax.axis_index("vid"), lax.axis_index("aud")
    return a % 4, v // 8, (a // 4) * 4 + (v // 2) % 4, v % 2


def device(place):
    x, y, z, c = place
    return ((y * 4 + z % 4) * 2 + c, (z // 4) * 4 + x)


def head_peer(place, k):
    x, y, z, c = place
    return x, y, (z + 2 * k + 16) % 16, c


def video_peer(place, k):
    x, y, z, c = place
    step = k // 2 if k >= 0 else -((-k) // 2)
    return (x + step + 4) % 4, y, z, (c + k) % 2 if k >= 0 else (c - k) % 2


def audio_peer(place, k):
    x, y, z, c = place
    step = k // 2 if k >= 0 else -((-k) // 2)
    return x, (y + step + 4) % 4, (z // 2) * 2 + (z + abs(k)) % 2, c


def send(src, dst, sems, n, place):
    return pltpu.make_async_remote_copy(
        src_ref=src,
        dst_ref=dst,
        send_sem=sems.at[0, n],
        recv_sem=sems.at[1, n],
        device_id=device(place),
        device_id_type=MESH,
    )


def weigh(side, first, tile, probs):
    lanes = pl.ds(first * BLOCK, WIDE * BLOCK)
    queries = tile[first : first + WIDE, 0, side].reshape(WIDE * BLOCK, DIM)

    def score(n):
        keys = tile[n : n + STEP, 0, 1 - side].reshape(STEP * BLOCK, DIM)
        return lax.dot_general(keys, queries, NT, preferred_element_type=F32)

    peak = None
    for n in range(0, 8, STEP):
        top = score(n).reshape(STEP * BLOCK // 8, 8, WIDE * BLOCK).max(0)
        peak = top if peak is None else jnp.maximum(peak, top)
    peak = peak.max(0, keepdims=True).astype(BF16).astype(F32)
    for n in range(0, 8, STEP):
        weight = jnp.exp2((score(n) - peak) * SCALE)
        probs[side, n * BLOCK : (n + STEP) * BLOCK, lanes] = weight.astype(BF16)
    return peak


def gather_values(side, first, peak, values_t, probs, out):
    num = jnp.dot(values_t[side], probs[side, :, first * BLOCK : (first + WIDE) * BLOCK], preferred_element_type=F32)
    total = num[DIM : DIM + 1]
    high = total.astype(BF16).astype(F32)
    row = lax.broadcasted_iota(jnp.int32, (16, WIDE * BLOCK), 0)
    stat = jnp.where(row == 0, peak, jnp.where(row == 1, high, jnp.where(row == 2, total - high, 0.0)))
    for s in range(WIDE):
        lanes = slice(s * BLOCK, (s + 1) * BLOCK)
        out[side, first + s, :BLOCK] = num[:DIM, lanes].astype(BF16)
        out[side, first + s, BLOCK:] = stat[:, lanes].astype(BF16)


def combine(side, part, back, mixed):
    def source(k):
        return part if k == 0 else back

    stats = [source(k)[side, k, BLOCK:].astype(F32) for k in range(8)]
    peaks = [s[0:1] for s in stats]
    top = peaks[0]
    for p in peaks[1:]:
        top = jnp.maximum(top, p)
    num = jnp.zeros((DIM, BLOCK), F32)
    total = jnp.zeros((1, BLOCK), F32)
    for k in range(8):
        gain = jnp.exp2((peaks[k] - top) * SCALE)
        total = total + gain * (stats[k][1:2] + stats[k][2:3])
        num = num + gain * source(k)[side, k, :BLOCK].astype(F32)
    mix = (num / total).T.astype(BF16)
    mixed[side] = mix.reshape(HEADS, ROWS, DIM)


def kernel(vm, vv, am, av, vproj, aproj, whole, vweights, aweights,
           tokens, staged, tile, values_t, probs, part, back, mixed, mixes,
           head_sems, gather_sems, return_sems, final_sems, local_sems):
    place = position()
    head = place[2] // 2
    loads = [
        pltpu.make_async_copy(array, tokens.at[n], local_sems.at[n]) for n, array in enumerate((vm, am, vv, av))
    ] + [
        pltpu.make_async_copy(vproj, vweights, local_sems.at[4]),
        pltpu.make_async_copy(aproj, aweights, local_sems.at[5]),
    ]
    for load in loads:
        load.start()

    barrier = pltpu.get_barrier_semaphore()
    for peer in (head_peer, video_peer, audio_peer):
        for k in range(1, 8):
            pl.semaphore_signal(barrier, inc=1, device_id=device(peer(place, k)), device_id_type=MESH)
    for n in range(4):
        loads[n].wait()
        for h in range(HEADS):
            staged[n // 2, h, n % 2] = tokens[n, :, h * DIM : (h + 1) * DIM]
    for kind in range(2):
        tile[0, kind, :, :ROWS] = staged[kind, head]
    values_t[:, DIM:] = jnp.ones((2, 16, TOKENS), BF16)
    pl.semaphore_wait(barrier, 21)

    sends = {}
    for kind in range(2):
        for k in FIRST:
            peer = head_peer(place, k)
            rows = pl.ds(ORDER.index(k) * ROWS, ROWS)
            sends[kind, k] = send(staged.at[kind, peer[2] // 2], tile.at[0, kind, :, rows], head_sems, 8 * kind + k, peer)
            sends[kind, k].start()

    gathers = {}
    for n, (kind, first, last) in enumerate(PARTS):
        for k in ORDER[first:last]:
            if k:
                sends[kind, k].wait_recv()
        rows = pl.ds(first * ROWS, (last - first) * ROWS)
        for k in (1, 4, 5, 2, 3, 6, 7):
            for side, peer in ((1, audio_peer), (0, video_peer)):
                sem = 16 * n + 8 * side + k
                gathers[n, side, k] = send(
                    tile.at[0, kind, side, rows], tile.at[k, kind, side, rows], gather_sems, sem, peer(place, k)
                )
                gathers[n, side, k].start()

    def arrive(kind):
        for n, side, k in gathers:
            if PARTS[n][0] == kind:
                gathers[n, side, k].wait_recv()

    arrive(0)
    peaks = {}
    for first in range(8 - WIDE, -1, -WIDE):
        for side in range(2):
            peaks[side, first] = weigh(side, first, tile, probs)
    arrive(1)
    for side in range(2):
        for k in range(8):
            values_t[side, :DIM, k * BLOCK : (k + 1) * BLOCK] = tile[k, 1, 1 - side].T
    returns = {}
    for first in range(8 - WIDE, -1, -WIDE):
        for side, peer in ((0, video_peer), (1, audio_peer)):
            gather_values(side, first, peaks[side, first], values_t, probs, part)
            for k in range(first, first + WIDE):
                if k:
                    returns[side, k] = send(part.at[side, k], back.at[side, k], return_sems, 8 * side + k, peer(place, -k))
                    returns[side, k].start()

    finals = {}
    for side in range(2):
        for k in range(1, 8):
            returns[side, k].wait_recv()
        combine(side, part, back, mixed)
        for k in (4, 3, 5, 2, 6, 1, 7):
            finals[side, k] = send(
                mixed.at[side, ORDER.index(k)], mixes.at[side, head], final_sems, 8 * side + k, head_peer(place, -k)
            )
            finals[side, k].start()
        mixes[side, head] = mixed[side, 0]
    for side in range(2):
        for k in range(1, 8):
            finals[side, k].wait_recv()
        for h in range(HEADS):
            whole[side, :, h * DIM : (h + 1) * DIM] = mixes[side, h]
    for load in loads[4:]:
        load.wait()
    for group in (sends, gathers, returns, finals):
        for s in group.values():
            s.wait_send()


def project(mix, vproj, aproj, vout, aout):
    for side, weights, out in ((0, vproj, vout), (1, aproj, aout)):
        out[...] = jnp.dot(mix[side], weights[...], preferred_element_type=F32).astype(BF16)


def shards(vm, vv, am, av, vproj, aproj):
    vmem = pl.BlockSpec(memory_space=pltpu.VMEM)
    hbm = pl.BlockSpec(memory_space=pltpu.HBM)
    held = pl.pallas_call(
        kernel,
        out_shape=[pltpu.VMEM((2, ROWS, WIDTH), BF16)] + [pltpu.VMEM((WIDTH, WIDTH), BF16)] * 2,
        in_specs=[hbm] * 6,
        out_specs=[vmem] * 3,
        scratch_shapes=[
            pltpu.VMEM((4, ROWS, WIDTH), BF16),
            pltpu.VMEM((2, HEADS, 2, ROWS, DIM), BF16),
            pltpu.VMEM((8, 2, 2, BLOCK, DIM), BF16),
            pltpu.VMEM((2, DIM + 16, TOKENS), BF16),
            pltpu.VMEM((2, TOKENS, TOKENS), BF16),
            pltpu.VMEM((2, 8, STAT, DIM), BF16),
            pltpu.VMEM((2, 8, STAT, DIM), BF16),
            pltpu.VMEM((2, HEADS, ROWS, DIM), BF16),
            pltpu.VMEM((2, HEADS, ROWS, DIM), BF16),
            pltpu.SemaphoreType.DMA((2, 16)),
            pltpu.SemaphoreType.DMA((2, 16 * len(PARTS))),
            pltpu.SemaphoreType.DMA((2, 16)),
            pltpu.SemaphoreType.DMA((2, 16)),
            pltpu.SemaphoreType.DMA((6,)),
        ],
        compiler_params=pltpu.CompilerParams(
            collective_id=0, has_side_effects=True, vmem_limit_bytes=KERNEL_VMEM
        ),
        name="attend",
    )(*(pltpu.with_memory_space_constraint(x, pltpu.HBM) for x in (vm, vv, am, av, vproj, aproj)))
    return pl.pallas_call(
        project,
        out_shape=[jax.ShapeDtypeStruct((ROWS, WIDTH), BF16)] * 2,
        in_specs=[vmem] * 3,
        out_specs=[vmem] * 2,
        compiler_params=pltpu.CompilerParams(vmem_limit_bytes=16 * 2**20),
        name="project",
    )(*(pltpu.with_memory_space_constraint(x, pltpu.VMEM) for x in held))


def solution(mesh):
    tokens = P(("vid", "aud"), None)
    return jax.shard_map(
        shards,
        mesh=mesh,
        in_specs=(tokens,) * 4 + (P(), P()),
        out_specs=(tokens, tokens),
        check_vma=False,
    )
```

```python
import math

import jax
import jax.numpy as jnp
from jax import lax
from jax.experimental import pallas as pl
from jax.experimental.pallas import tpu as pltpu
from jax.sharding import PartitionSpec as P

MESH = pl.DeviceIdType.MESH
HEADS = 8
DIM = 128
ROWS = 16
BLOCK = HEADS * ROWS
TOKENS = 8 * BLOCK
WIDTH = HEADS * DIM
STAT = BLOCK + 16
KERNEL_VMEM = 32 * 2**20
FIRST = (4, 1, 7, 2, 6, 3, 5)
WIDE = 4
STEP = 2
ORDER = (0, 1, 7, 2, 6, 3, 5, 4)
PARTS = ((0, 0, 5), (0, 5, 8), (1, 0, 5), (1, 5, 8))
SCALE = DIM ** (-0.5) * math.log2(math.e)
F32, BF16 = jnp.float32, jnp.bfloat16
NT = (((1,), (1,)), ((), ()))


def position():
    v, a = lax.axis_index("vid"), lax.axis_index("aud")
    return a % 4, v // 8, (a // 4) * 4 + (v // 2) % 4, v % 2


def device(place):
    x, y, z, c = place
    return ((y * 4 + z % 4) * 2 + c, (z // 4) * 4 + x)


def head_peer(place, k):
    x, y, z, c = place
    return x, y, (z + 2 * k + 16) % 16, c


def video_peer(place, k):
    x, y, z, c = place
    step = k // 2 if k >= 0 else -((-k) // 2)
    return (x + step + 4) % 4, y, z, (c + k) % 2 if k >= 0 else (c - k) % 2


def audio_peer(place, k):
    x, y, z, c = place
    step = k // 2 if k >= 0 else -((-k) // 2)
    return x, (y + step + 4) % 4, (z // 2) * 2 + (z + abs(k)) % 2, c


def send(src, dst, sems, n, place):
    return pltpu.make_async_remote_copy(
        src_ref=src,
        dst_ref=dst,
        send_sem=sems.at[0, n],
        recv_sem=sems.at[1, n],
        device_id=device(place),
        device_id_type=MESH,
    )


def weigh(tile, tops, probs):
    wide, step = WIDE * BLOCK, STEP * BLOCK

    def score(n, first):
        keys = tile[n : n + STEP, 0, 1].reshape(step, DIM)
        queries = tile[first : first + WIDE, 0, 0].reshape(wide, DIM)
        return lax.dot_general(keys, queries, NT, preferred_element_type=F32)

    peaks = [{}, {}]
    for first in range(0, 8, WIDE):
        peak = None
        for n in range(0, 8, STEP):
            tops_of = pl.ds(n * BLOCK, step)
            scores = score(n, first)
            top = scores.reshape(step // 8, 8, wide).max(0)
            peak = top if peak is None else jnp.maximum(peak, top)
            top = scores[:, :BLOCK]
            for s in range(1, WIDE):
                top = jnp.maximum(top, scores[:, s * BLOCK : (s + 1) * BLOCK])
            tops[tops_of] = jnp.maximum(tops[tops_of], top) if first else top
        peaks[0][first] = peak.max(0, keepdims=True).astype(BF16).astype(F32)
    for n in range(0, 8, STEP):
        rows = slice(n * BLOCK, n * BLOCK + step)
        across = tops[rows].max(1, keepdims=True).astype(BF16).astype(F32)
        for first in range(0, 8, WIDE):
            lanes = slice(first * BLOCK, first * BLOCK + wide)
            scores = score(n, first)
            probs[0, rows, lanes] = jnp.exp2((scores - peaks[0][first]) * SCALE).astype(BF16)
            probs[1, rows, lanes] = jnp.exp2((scores - across) * SCALE).astype(BF16)
    for first in range(0, 8, WIDE):
        peaks[1][first] = jnp.concatenate(
            [tops[n * BLOCK : (n + 1) * BLOCK].T.max(0, keepdims=True) for n in range(first, first + WIDE)], axis=1
        ).astype(BF16).astype(F32)
    return peaks


def gather_values(side, first, peak, values_t, probs, out):
    tokens = slice(first * BLOCK, (first + WIDE) * BLOCK)
    if side:
        num = lax.dot_general(values_t[1], probs[1, tokens], NT, preferred_element_type=F32)
    else:
        num = jnp.dot(values_t[0], probs[0, :, tokens], preferred_element_type=F32)
    total = num[DIM : DIM + 1]
    high = total.astype(BF16).astype(F32)
    row = lax.broadcasted_iota(jnp.int32, (16, WIDE * BLOCK), 0)
    stat = jnp.where(row == 0, peak, jnp.where(row == 1, high, jnp.where(row == 2, total - high, 0.0)))
    for s in range(WIDE):
        lanes = slice(s * BLOCK, (s + 1) * BLOCK)
        out[side, first + s, :BLOCK] = num[:DIM, lanes].astype(BF16)
        out[side, first + s, BLOCK:] = stat[:, lanes].astype(BF16)


def combine(side, part, back, mixed):
    def source(k):
        return part if k == 0 else back

    stats = [source(k)[side, k, BLOCK:].astype(F32) for k in range(8)]
    peaks = [s[0:1] for s in stats]
    top = peaks[0]
    for p in peaks[1:]:
        top = jnp.maximum(top, p)
    num = jnp.zeros((DIM, BLOCK), F32)
    total = jnp.zeros((1, BLOCK), F32)
    for k in range(8):
        gain = jnp.exp2((peaks[k] - top) * SCALE)
        total = total + gain * (stats[k][1:2] + stats[k][2:3])
        num = num + gain * source(k)[side, k, :BLOCK].astype(F32)
    mix = (num / total).T.astype(BF16)
    mixed[side] = mix.reshape(HEADS, ROWS, DIM)


def kernel(vm, vv, am, av, vproj, aproj, whole, vweights, aweights,
           tokens, staged, tile, values_t, tops, probs, part, back, mixed, mixes,
           head_sems, gather_sems, return_sems, final_sems, local_sems):
    place = position()
    head = place[2] // 2
    loads = [
        pltpu.make_async_copy(array, tokens.at[n], local_sems.at[n]) for n, array in enumerate((vm, am, vv, av))
    ] + [
        pltpu.make_async_copy(vproj, vweights, local_sems.at[4]),
        pltpu.make_async_copy(aproj, aweights, local_sems.at[5]),
    ]
    for load in loads:
        load.start()

    barrier = pltpu.get_barrier_semaphore()
    for peer in (head_peer, video_peer, audio_peer):
        for k in range(1, 8):
            pl.semaphore_signal(barrier, inc=1, device_id=device(peer(place, k)), device_id_type=MESH)
    for n in range(4):
        loads[n].wait()
        for h in range(HEADS):
            staged[n // 2, h, n % 2] = tokens[n, :, h * DIM : (h + 1) * DIM]
    for kind in range(2):
        tile[0, kind, :, :ROWS] = staged[kind, head]
    values_t[:, DIM:] = jnp.ones((2, 16, TOKENS), BF16)
    pl.semaphore_wait(barrier, 21)

    sends = {}
    for kind in range(2):
        for k in FIRST:
            peer = head_peer(place, k)
            rows = pl.ds(ORDER.index(k) * ROWS, ROWS)
            sends[kind, k] = send(staged.at[kind, peer[2] // 2], tile.at[0, kind, :, rows], head_sems, 8 * kind + k, peer)
            sends[kind, k].start()

    gathers = {}
    for n, (kind, first, last) in enumerate(PARTS):
        for k in ORDER[first:last]:
            if k:
                sends[kind, k].wait_recv()
        rows = pl.ds(first * ROWS, (last - first) * ROWS)
        for k in (1, 4, 5, 2, 3, 6, 7):
            for side, peer in ((1, audio_peer), (0, video_peer)):
                sem = 16 * n + 8 * side + k
                gathers[n, side, k] = send(
                    tile.at[0, kind, side, rows], tile.at[k, kind, side, rows], gather_sems, sem, peer(place, k)
                )
                gathers[n, side, k].start()

    def arrive(kind):
        for n, side, k in gathers:
            if PARTS[n][0] == kind:
                gathers[n, side, k].wait_recv()

    arrive(0)
    peaks = weigh(tile, tops, probs)
    arrive(1)
    for side in range(2):
        for k in range(8):
            values_t[side, :DIM, k * BLOCK : (k + 1) * BLOCK] = tile[k, 1, 1 - side].T
    returns = {}
    for first in range(8 - WIDE, -1, -WIDE):
        for side, peer in ((0, video_peer), (1, audio_peer)):
            gather_values(side, first, peaks[side][first], values_t, probs, part)
            for k in range(first, first + WIDE):
                if k:
                    returns[side, k] = send(part.at[side, k], back.at[side, k], return_sems, 8 * side + k, peer(place, -k))
                    returns[side, k].start()

    finals = {}
    for side in (1, 0):
        for k in range(1, 8):
            returns[side, k].wait_recv()
        combine(side, part, back, mixed)
        for k in (4, 3, 5, 2, 6, 1, 7):
            finals[side, k] = send(
                mixed.at[side, ORDER.index(k)], mixes.at[side, head], final_sems, 8 * side + k, head_peer(place, -k)
            )
            finals[side, k].start()
        mixes[side, head] = mixed[side, 0]
    for side in range(2):
        for k in range(1, 8):
            finals[side, k].wait_recv()
        for h in range(HEADS):
            whole[side, :, h * DIM : (h + 1) * DIM] = mixes[side, h]
    for load in loads[4:]:
        load.wait()
    for group in (sends, gathers, returns, finals):
        for s in group.values():
            s.wait_send()


def project(mix, vproj, aproj, vout, aout):
    for side, weights, out in ((0, vproj, vout), (1, aproj, aout)):
        out[...] = jnp.dot(mix[side], weights[...], preferred_element_type=F32).astype(BF16)


def shards(vm, vv, am, av, vproj, aproj):
    vmem = pl.BlockSpec(memory_space=pltpu.VMEM)
    hbm = pl.BlockSpec(memory_space=pltpu.HBM)
    held = pl.pallas_call(
        kernel,
        out_shape=[pltpu.VMEM((2, ROWS, WIDTH), BF16)] + [pltpu.VMEM((WIDTH, WIDTH), BF16)] * 2,
        in_specs=[hbm] * 6,
        out_specs=[vmem] * 3,
        scratch_shapes=[
            pltpu.VMEM((4, ROWS, WIDTH), BF16),
            pltpu.VMEM((2, HEADS, 2, ROWS, DIM), BF16),
            pltpu.VMEM((8, 2, 2, BLOCK, DIM), BF16),
            pltpu.VMEM((2, DIM + 16, TOKENS), BF16),
            pltpu.VMEM((TOKENS, BLOCK), F32),
            pltpu.VMEM((2, TOKENS, TOKENS), BF16),
            pltpu.VMEM((2, 8, STAT, DIM), BF16),
            pltpu.VMEM((2, 8, STAT, DIM), BF16),
            pltpu.VMEM((2, HEADS, ROWS, DIM), BF16),
            pltpu.VMEM((2, HEADS, ROWS, DIM), BF16),
            pltpu.SemaphoreType.DMA((2, 16)),
            pltpu.SemaphoreType.DMA((2, 16 * len(PARTS))),
            pltpu.SemaphoreType.DMA((2, 16)),
            pltpu.SemaphoreType.DMA((2, 16)),
            pltpu.SemaphoreType.DMA((6,)),
        ],
        compiler_params=pltpu.CompilerParams(
            collective_id=0, has_side_effects=True, vmem_limit_bytes=KERNEL_VMEM
        ),
        name="attend",
    )(*(pltpu.with_memory_space_constraint(x, pltpu.HBM) for x in (vm, vv, am, av, vproj, aproj)))
    return pl.pallas_call(
        project,
        out_shape=[jax.ShapeDtypeStruct((ROWS, WIDTH), BF16)] * 2,
        in_specs=[vmem] * 3,
        out_specs=[vmem] * 2,
        compiler_params=pltpu.CompilerParams(vmem_limit_bytes=16 * 2**20),
        name="project",
    )(*(pltpu.with_memory_space_constraint(x, pltpu.VMEM) for x in held))


def solution(mesh):
    tokens = P(("vid", "aud"), None)
    return jax.shard_map(
        shards,
        mesh=mesh,
        in_specs=(tokens,) * 4 + (P(), P()),
        out_specs=(tokens, tokens),
        check_vma=False,
    )
```

```python
import math

import jax
import jax.numpy as jnp
from jax import lax
from jax.experimental import pallas as pl
from jax.experimental.pallas import tpu as pltpu
from jax.sharding import PartitionSpec as P

MESH = pl.DeviceIdType.MESH
HEADS = 8
DIM = 128
ROWS = 16
BLOCK = HEADS * ROWS
TOKENS = 8 * BLOCK
WIDTH = HEADS * DIM
STAT = BLOCK + 16
KERNEL_VMEM = 32 * 2**20
WIDE = 4
STEP = 2
ORDER = (0, 1, 7, 2, 6, 3, 5, 4)
PARTS = ((None, 0, 5), (0, 5, 8), (1, 5, 8))
SCALE = DIM ** (-0.5) * math.log2(math.e)
F32, BF16 = jnp.float32, jnp.bfloat16
NT = (((1,), (1,)), ((), ()))


def position():
    v, a = lax.axis_index("vid"), lax.axis_index("aud")
    return a % 4, v // 8, (a // 4) * 4 + (v // 2) % 4, v % 2


def device(place):
    x, y, z, c = place
    return ((y * 4 + z % 4) * 2 + c, (z // 4) * 4 + x)


def head_peer(place, k):
    x, y, z, c = place
    return x, y, (z + 2 * k + 16) % 16, c


def video_peer(place, k):
    x, y, z, c = place
    step = k // 2 if k >= 0 else -((-k) // 2)
    return (x + step + 4) % 4, y, z, (c + k) % 2 if k >= 0 else (c - k) % 2


def audio_peer(place, k):
    x, y, z, c = place
    step = k // 2 if k >= 0 else -((-k) // 2)
    return x, (y + step + 4) % 4, (z // 2) * 2 + (z + abs(k)) % 2, c


def send(src, dst, sems, n, place):
    return pltpu.make_async_remote_copy(
        src_ref=src,
        dst_ref=dst,
        send_sem=sems.at[0, n],
        recv_sem=sems.at[1, n],
        device_id=device(place),
        device_id_type=MESH,
    )


def weigh(tile, tops, probs):
    wide, step = WIDE * BLOCK, STEP * BLOCK

    def score(n, first):
        keys = tile[n : n + STEP, 0, 1].reshape(step, DIM)
        queries = tile[first : first + WIDE, 0, 0].reshape(wide, DIM)
        return lax.dot_general(keys, queries, NT, preferred_element_type=F32)

    peaks = [{}, {}]
    for first in range(0, 8, WIDE):
        peak = None
        for n in range(0, 8, STEP):
            tops_of = pl.ds(n * BLOCK, step)
            scores = score(n, first)
            top = scores.reshape(step // 8, 8, wide).max(0)
            peak = top if peak is None else jnp.maximum(peak, top)
            top = scores[:, :BLOCK]
            for s in range(1, WIDE):
                top = jnp.maximum(top, scores[:, s * BLOCK : (s + 1) * BLOCK])
            tops[tops_of] = jnp.maximum(tops[tops_of], top) if first else top
        peaks[0][first] = peak.max(0, keepdims=True).astype(BF16).astype(F32)
    for n in range(0, 8, STEP):
        rows = slice(n * BLOCK, n * BLOCK + step)
        across = tops[rows].max(1, keepdims=True).astype(BF16).astype(F32)
        for first in range(0, 8, WIDE):
            lanes = slice(first * BLOCK, first * BLOCK + wide)
            scores = score(n, first)
            probs[0, rows, lanes] = jnp.exp2((scores - peaks[0][first]) * SCALE).astype(BF16)
            probs[1, rows, lanes] = jnp.exp2((scores - across) * SCALE).astype(BF16)
    for first in range(0, 8, WIDE):
        peaks[1][first] = jnp.concatenate(
            [tops[n * BLOCK : (n + 1) * BLOCK].T.max(0, keepdims=True) for n in range(first, first + WIDE)], axis=1
        ).astype(BF16).astype(F32)
    return peaks


def gather_values(side, first, peak, values_t, probs, out):
    tokens = slice(first * BLOCK, (first + WIDE) * BLOCK)
    if side:
        num = lax.dot_general(values_t[1], probs[1, tokens], NT, preferred_element_type=F32)
    else:
        num = jnp.dot(values_t[0], probs[0, :, tokens], preferred_element_type=F32)
    total = num[DIM : DIM + 1]
    high = total.astype(BF16).astype(F32)
    row = lax.broadcasted_iota(jnp.int32, (16, WIDE * BLOCK), 0)
    stat = jnp.where(row == 0, peak, jnp.where(row == 1, high, jnp.where(row == 2, total - high, 0.0)))
    for s in range(WIDE):
        lanes = slice(s * BLOCK, (s + 1) * BLOCK)
        out[side, first + s, :BLOCK] = num[:DIM, lanes].astype(BF16)
        out[side, first + s, BLOCK:] = stat[:, lanes].astype(BF16)


def combine(side, part, back, mixed):
    def source(k):
        return part if k == 0 else back

    stats = [source(k)[side, k, BLOCK:].astype(F32) for k in range(8)]
    peaks = [s[0:1] for s in stats]
    top = peaks[0]
    for p in peaks[1:]:
        top = jnp.maximum(top, p)
    num = jnp.zeros((DIM, BLOCK), F32)
    total = jnp.zeros((1, BLOCK), F32)
    for k in range(8):
        gain = jnp.exp2((peaks[k] - top) * SCALE)
        total = total + gain * (stats[k][1:2] + stats[k][2:3])
        num = num + gain * source(k)[side, k, :BLOCK].astype(F32)
    mix = (num / total).T.astype(BF16)
    mixed[side] = mix.reshape(HEADS, ROWS, DIM)


def kernel(vm, vv, am, av, vproj, aproj, whole, vweights, aweights,
           tokens, staged, passing, tile, values_t, tops, probs, part, back, mixed, mixes,
           pass_sems, head_sems, gather_sems, return_sems, final_sems, local_sems):
    place = position()
    head = place[2] // 2
    loads = [
        pltpu.make_async_copy(array, tokens.at[n], local_sems.at[n]) for n, array in enumerate((vm, am, vv, av))
    ] + [
        pltpu.make_async_copy(vproj, vweights, local_sems.at[4]),
        pltpu.make_async_copy(aproj, aweights, local_sems.at[5]),
    ]
    for load in loads:
        load.start()

    barrier = pltpu.get_barrier_semaphore()
    greeted = [(head_peer, k) for k in (2, 6, 1, 7)] + [(peer, k) for peer in (video_peer, audio_peer) for k in range(1, 8)]
    for peer, k in greeted:
        pl.semaphore_signal(barrier, inc=1, device_id=device(peer(place, k)), device_id_type=MESH)
    for n in range(4):
        loads[n].wait()
        for h in range(HEADS):
            staged[n // 2, h, n % 2] = tokens[n, :, h * DIM : (h + 1) * DIM]
    for kind in range(2):
        tile[0, kind, :, :ROWS] = staged[kind, head]
    values_t[:, DIM:] = jnp.ones((2, 16, TOKENS), BF16)
    pl.semaphore_wait(barrier, len(greeted))

    def rows_of(k):
        return pl.ds(ORDER.index(k) * ROWS, ROWS)

    def columns(kind, k):
        return staged.at[kind, (head + k) % HEADS]

    legs, sends = {}, {}
    for kind in (0,):
        for n, (src, dst, via) in enumerate((
            (columns(kind, 4).at[0], passing.at[kind, 2, 0], 2),
            (columns(kind, 4).at[1], passing.at[kind, 2, 1], -2),
            (columns(kind, 3), passing.at[kind, 0], 2),
            (columns(kind, 5), passing.at[kind, 1], -2),
        )):
            legs[kind, n] = send(src, dst, pass_sems, 4 * kind + n, head_peer(place, via))
            legs[kind, n].start()
    for k in (1, 7, 2, 6):
        sends[k] = send(
            staged.at[:, (head + k) % HEADS], tile.at[0, :, :, rows_of(k)], head_sems, k, head_peer(place, k)
        )
        sends[k].start()
    for kind in (1,):
        for n, (src, dst, via) in enumerate((
            (columns(kind, 4).at[0], passing.at[kind, 2, 0], 2),
            (columns(kind, 4).at[1], passing.at[kind, 2, 1], -2),
            (columns(kind, 3), passing.at[kind, 0], 2),
            (columns(kind, 5), passing.at[kind, 1], -2),
        )):
            legs[kind, n] = send(src, dst, pass_sems, 4 * kind + n, head_peer(place, via))
            legs[kind, n].start()
    for kind in range(2):
        for n, (src, dst, to) in enumerate((
            (passing.at[kind, 2, 0], tile.at[0, kind, 0, rows_of(4)], 2),
            (passing.at[kind, 2, 1], tile.at[0, kind, 1, rows_of(4)], -2),
            (passing.at[kind, 0], tile.at[0, kind, :, rows_of(3)], 1),
            (passing.at[kind, 1], tile.at[0, kind, :, rows_of(5)], -1),
        )):
            legs[kind, n].wait_recv()
            sends[kind, n] = send(src, dst, head_sems, 8 + 4 * kind + n, head_peer(place, to))
            sends[kind, n].start()

    gathers = {}
    for n, (kind, first, last) in enumerate(PARTS):
        for key in (2, 6, 1, 7) if kind is None else ((kind, 0), (kind, 1), (kind, 2), (kind, 3)):
            sends[key].wait_recv()
        rows = pl.ds(first * ROWS, (last - first) * ROWS)
        kinds = slice(None) if kind is None else kind
        for k in (1, 4, 5, 2, 3, 6, 7):
            for side, peer in ((1, audio_peer), (0, video_peer)):
                sem = 16 * n + 8 * side + k
                gathers[n, side, k] = send(
                    tile.at[0, kinds, side, rows], tile.at[k, kinds, side, rows], gather_sems, sem, peer(place, k)
                )
                gathers[n, side, k].start()

    def arrive(kind):
        for n, side, k in gathers:
            if (PARTS[n][0] or 0) == kind:
                gathers[n, side, k].wait_recv()

    arrive(0)
    peaks = weigh(tile, tops, probs)
    arrive(1)
    for side in range(2):
        for k in range(8):
            values_t[side, :DIM, k * BLOCK : (k + 1) * BLOCK] = tile[k, 1, 1 - side].T
    returns = {}
    for first in range(8 - WIDE, -1, -WIDE):
        for side, peer in ((0, video_peer), (1, audio_peer)):
            gather_values(side, first, peaks[side][first], values_t, probs, part)
            for k in range(first, first + WIDE):
                if k:
                    returns[side, k] = send(part.at[side, k], back.at[side, k], return_sems, 8 * side + k, peer(place, -k))
                    returns[side, k].start()

    finals = {}
    for side in (1, 0):
        for k in range(1, 8):
            returns[side, k].wait_recv()
        combine(side, part, back, mixed)
        for k in (4, 3, 5, 2, 6, 1, 7):
            finals[side, k] = send(
                mixed.at[side, ORDER.index(k)], mixes.at[side, head], final_sems, 8 * side + k, head_peer(place, -k)
            )
            finals[side, k].start()
        mixes[side, head] = mixed[side, 0]
    for side in range(2):
        for k in range(1, 8):
            finals[side, k].wait_recv()
        for h in range(HEADS):
            whole[side, :, h * DIM : (h + 1) * DIM] = mixes[side, h]
    for load in loads[4:]:
        load.wait()
    for group in (legs, sends, gathers, returns, finals):
        for s in group.values():
            s.wait_send()


def project(mix, vproj, aproj, vout, aout):
    for side, weights, out in ((0, vproj, vout), (1, aproj, aout)):
        out[...] = jnp.dot(mix[side], weights[...], preferred_element_type=F32).astype(BF16)


def shards(vm, vv, am, av, vproj, aproj):
    vmem = pl.BlockSpec(memory_space=pltpu.VMEM)
    hbm = pl.BlockSpec(memory_space=pltpu.HBM)
    held = pl.pallas_call(
        kernel,
        out_shape=[pltpu.VMEM((2, ROWS, WIDTH), BF16)] + [pltpu.VMEM((WIDTH, WIDTH), BF16)] * 2,
        in_specs=[hbm] * 6,
        out_specs=[vmem] * 3,
        scratch_shapes=[
            pltpu.VMEM((4, ROWS, WIDTH), BF16),
            pltpu.VMEM((2, HEADS, 2, ROWS, DIM), BF16),
            pltpu.VMEM((2, 3, 2, ROWS, DIM), BF16),
            pltpu.VMEM((8, 2, 2, BLOCK, DIM), BF16),
            pltpu.VMEM((2, DIM + 16, TOKENS), BF16),
            pltpu.VMEM((TOKENS, BLOCK), F32),
            pltpu.VMEM((2, TOKENS, TOKENS), BF16),
            pltpu.VMEM((2, 8, STAT, DIM), BF16),
            pltpu.VMEM((2, 8, STAT, DIM), BF16),
            pltpu.VMEM((2, HEADS, ROWS, DIM), BF16),
            pltpu.VMEM((2, HEADS, ROWS, DIM), BF16),
            pltpu.SemaphoreType.DMA((2, 8)),
            pltpu.SemaphoreType.DMA((2, 16)),
            pltpu.SemaphoreType.DMA((2, 16 * len(PARTS))),
            pltpu.SemaphoreType.DMA((2, 16)),
            pltpu.SemaphoreType.DMA((2, 16)),
            pltpu.SemaphoreType.DMA((6,)),
        ],
        compiler_params=pltpu.CompilerParams(
            collective_id=0, has_side_effects=True, vmem_limit_bytes=KERNEL_VMEM
        ),
        name="attend",
    )(*(pltpu.with_memory_space_constraint(x, pltpu.HBM) for x in (vm, vv, am, av, vproj, aproj)))
    return pl.pallas_call(
        project,
        out_shape=[jax.ShapeDtypeStruct((ROWS, WIDTH), BF16)] * 2,
        in_specs=[vmem] * 3,
        out_specs=[vmem] * 2,
        compiler_params=pltpu.CompilerParams(vmem_limit_bytes=16 * 2**20),
        name="project",
    )(*(pltpu.with_memory_space_constraint(x, pltpu.VMEM) for x in held))


def solution(mesh):
    tokens = P(("vid", "aud"), None)
    return jax.shard_map(
        shards,
        mesh=mesh,
        in_specs=(tokens,) * 4 + (P(), P()),
        out_specs=(tokens, tokens),
        check_vma=False,
    )
```

```python
import math

import jax
import jax.numpy as jnp
from jax import lax
from jax.experimental import pallas as pl
from jax.experimental.pallas import tpu as pltpu
from jax.sharding import PartitionSpec as P

MESH = pl.DeviceIdType.MESH
HEADS = 8
DIM = 128
ROWS = 16
BLOCK = HEADS * ROWS
TOKENS = 8 * BLOCK
WIDTH = HEADS * DIM
STAT = BLOCK + 16
KERNEL_VMEM = 32 * 2**20
WIDE = 4
STEP = 2
ORDER = (0, 1, 7, 2, 6, 3, 5, 4)
PARTS = ((None, 0, 5), (0, 5, 8), (1, 5, 8))
SCALE = DIM ** (-0.5) * math.log2(math.e)
F32, BF16 = jnp.float32, jnp.bfloat16
NT = (((1,), (1,)), ((), ()))


def position():
    v, a = lax.axis_index("vid"), lax.axis_index("aud")
    return a % 4, v // 8, (a // 4) * 4 + (v // 2) % 4, v % 2


def device(place):
    x, y, z, c = place
    return ((y * 4 + z % 4) * 2 + c, (z // 4) * 4 + x)


def head_peer(place, k):
    x, y, z, c = place
    return x, y, (z + 2 * k + 16) % 16, c


def video_peer(place, k):
    x, y, z, c = place
    step = k // 2 if k >= 0 else -((-k) // 2)
    return (x + step + 4) % 4, y, z, (c + k) % 2 if k >= 0 else (c - k) % 2


def audio_peer(place, k):
    x, y, z, c = place
    step = k // 2 if k >= 0 else -((-k) // 2)
    return x, (y + step + 4) % 4, (z // 2) * 2 + (z + abs(k)) % 2, c


def send(src, dst, sems, n, place):
    return pltpu.make_async_remote_copy(
        src_ref=src,
        dst_ref=dst,
        send_sem=sems.at[0, n],
        recv_sem=sems.at[1, n],
        device_id=device(place),
        device_id_type=MESH,
    )


def weigh(tile, tops, probs):
    wide, step = WIDE * BLOCK, STEP * BLOCK

    def score(n, first):
        keys = tile[n : n + STEP, 0, 1].reshape(step, DIM)
        queries = tile[first : first + WIDE, 0, 0].reshape(wide, DIM)
        return lax.dot_general(keys, queries, NT, preferred_element_type=F32)

    peaks = [{}, {}]
    for first in range(0, 8, WIDE):
        peak = None
        for n in range(0, 8, STEP):
            tops_of = pl.ds(n * BLOCK, step)
            scores = score(n, first)
            top = scores.reshape(step // 8, 8, wide).max(0)
            peak = top if peak is None else jnp.maximum(peak, top)
            top = scores[:, :BLOCK]
            for s in range(1, WIDE):
                top = jnp.maximum(top, scores[:, s * BLOCK : (s + 1) * BLOCK])
            tops[tops_of] = jnp.maximum(tops[tops_of], top) if first else top
        peaks[0][first] = peak.max(0, keepdims=True).astype(BF16).astype(F32)
    for n in range(0, 8, STEP):
        rows = slice(n * BLOCK, n * BLOCK + step)
        across = tops[rows].max(1, keepdims=True).astype(BF16).astype(F32)
        for first in range(0, 8, WIDE):
            lanes = slice(first * BLOCK, first * BLOCK + wide)
            scores = score(n, first)
            probs[0, rows, lanes] = jnp.exp2((scores - peaks[0][first]) * SCALE).astype(BF16)
            probs[1, rows, lanes] = jnp.exp2((scores - across) * SCALE).astype(BF16)
    for first in range(0, 8, WIDE):
        peaks[1][first] = jnp.concatenate(
            [tops[n * BLOCK : (n + 1) * BLOCK].T.max(0, keepdims=True) for n in range(first, first + WIDE)], axis=1
        ).astype(BF16).astype(F32)
    return peaks


def gather_values(side, first, peak, values_t, probs, out):
    tokens = slice(first * BLOCK, (first + WIDE) * BLOCK)
    if side:
        num = lax.dot_general(values_t[1], probs[1, tokens], NT, preferred_element_type=F32)
    else:
        num = jnp.dot(values_t[0], probs[0, :, tokens], preferred_element_type=F32)
    total = num[DIM : DIM + 1]
    high = total.astype(BF16).astype(F32)
    row = lax.broadcasted_iota(jnp.int32, (16, WIDE * BLOCK), 0)
    stat = jnp.where(row == 0, peak, jnp.where(row == 1, high, jnp.where(row == 2, total - high, 0.0)))
    for s in range(WIDE):
        lanes = slice(s * BLOCK, (s + 1) * BLOCK)
        out[side, first + s, :BLOCK] = num[:DIM, lanes].astype(BF16)
        out[side, first + s, BLOCK:] = stat[:, lanes].astype(BF16)


def combine(side, part, back, mixed):
    def source(k):
        return part if k == 0 else back

    stats = [source(k)[side, k, BLOCK:].astype(F32) for k in range(8)]
    peaks = [s[0:1] for s in stats]
    top = peaks[0]
    for p in peaks[1:]:
        top = jnp.maximum(top, p)
    num = jnp.zeros((DIM, BLOCK), F32)
    total = jnp.zeros((1, BLOCK), F32)
    for k in range(8):
        gain = jnp.exp2((peaks[k] - top) * SCALE)
        total = total + gain * (stats[k][1:2] + stats[k][2:3])
        num = num + gain * source(k)[side, k, :BLOCK].astype(F32)
    mix = (num / total).T.astype(BF16)
    mixed[side] = mix.reshape(HEADS, ROWS, DIM)


def kernel(vm, vv, am, av, vproj, aproj, whole, vweights, aweights,
           tokens, staged, passing, tile, values_t, tops, probs, part, back, mixed, mixes,
           pass_sems, head_sems, gather_sems, return_sems, final_sems, local_sems):
    place = position()
    head = place[2] // 2
    barrier = pltpu.get_barrier_semaphore()
    greeted = [(head_peer, k) for k in (2, 6, 1, 7)] + [(peer, k) for peer in (video_peer, audio_peer) for k in range(1, 8)]
    for peer, k in greeted:
        pl.semaphore_signal(barrier, inc=1, device_id=device(peer(place, k)), device_id_type=MESH)
    loads = [
        pltpu.make_async_copy(array, tokens.at[n], local_sems.at[n]) for n, array in enumerate((vm, am, vv, av))
    ] + [
        pltpu.make_async_copy(vproj, vweights, local_sems.at[4]),
        pltpu.make_async_copy(aproj, aweights, local_sems.at[5]),
    ]
    for load in loads:
        load.start()

    for n in range(4):
        loads[n].wait()
        for h in range(HEADS):
            staged[n // 2, h, n % 2] = tokens[n, :, h * DIM : (h + 1) * DIM]
    for kind in range(2):
        tile[0, kind, :, :ROWS] = staged[kind, head]
    values_t[:, DIM:] = jnp.ones((2, 16, TOKENS), BF16)
    pl.semaphore_wait(barrier, len(greeted))

    def rows_of(k):
        return pl.ds(ORDER.index(k) * ROWS, ROWS)

    def columns(kind, k):
        return staged.at[kind, (head + k) % HEADS]

    legs, sends = {}, {}
    for kind in (0,):
        for n, (src, dst, via) in enumerate((
            (columns(kind, 4).at[0], passing.at[kind, 2, 0], 2),
            (columns(kind, 4).at[1], passing.at[kind, 2, 1], -2),
            (columns(kind, 3), passing.at[kind, 0], 2),
            (columns(kind, 5), passing.at[kind, 1], -2),
        )):
            legs[kind, n] = send(src, dst, pass_sems, 4 * kind + n, head_peer(place, via))
            legs[kind, n].start()
    for k in (1, 7, 2, 6):
        sends[k] = send(
            staged.at[:, (head + k) % HEADS], tile.at[0, :, :, rows_of(k)], head_sems, k, head_peer(place, k)
        )
        sends[k].start()
    for kind in (1,):
        for n, (src, dst, via) in enumerate((
            (columns(kind, 4).at[0], passing.at[kind, 2, 0], 2),
            (columns(kind, 4).at[1], passing.at[kind, 2, 1], -2),
            (columns(kind, 3), passing.at[kind, 0], 2),
            (columns(kind, 5), passing.at[kind, 1], -2),
        )):
            legs[kind, n] = send(src, dst, pass_sems, 4 * kind + n, head_peer(place, via))
            legs[kind, n].start()
    for kind in range(2):
        for n, (src, dst, to) in enumerate((
            (passing.at[kind, 2, 0], tile.at[0, kind, 0, rows_of(4)], 2),
            (passing.at[kind, 2, 1], tile.at[0, kind, 1, rows_of(4)], -2),
            (passing.at[kind, 0], tile.at[0, kind, :, rows_of(3)], 1),
            (passing.at[kind, 1], tile.at[0, kind, :, rows_of(5)], -1),
        )):
            legs[kind, n].wait_recv()
            sends[kind, n] = send(src, dst, head_sems, 8 + 4 * kind + n, head_peer(place, to))
            sends[kind, n].start()

    gathers = {}
    for n, (kind, first, last) in enumerate(PARTS):
        for key in (2, 6, 1, 7) if kind is None else ((kind, 0), (kind, 1), (kind, 2), (kind, 3)):
            sends[key].wait_recv()
        rows = pl.ds(first * ROWS, (last - first) * ROWS)
        kinds = slice(None) if kind is None else kind
        for k in (5, 4, 3, 7, 2, 6, 1):
            for side, peer in ((1, audio_peer), (0, video_peer)):
                sem = 16 * n + 8 * side + k
                gathers[n, side, k] = send(
                    tile.at[0, kinds, side, rows], tile.at[k, kinds, side, rows], gather_sems, sem, peer(place, k)
                )
                gathers[n, side, k].start()

    def arrive(kind):
        for n, side, k in gathers:
            if (PARTS[n][0] or 0) == kind:
                gathers[n, side, k].wait_recv()

    arrive(0)
    peaks = weigh(tile, tops, probs)
    arrive(1)
    for side in range(2):
        for k in range(8):
            values_t[side, :DIM, k * BLOCK : (k + 1) * BLOCK] = tile[k, 1, 1 - side].T
    returns = {}
    for first in range(8 - WIDE, -1, -WIDE):
        for side, peer in ((0, video_peer), (1, audio_peer)):
            gather_values(side, first, peaks[side][first], values_t, probs, part)
            for k in (first + 1, first, first + 3, first + 2):
                if k:
                    returns[side, k] = send(part.at[side, k], back.at[side, k], return_sems, 8 * side + k, peer(place, -k))
                    returns[side, k].start()

    finals = {}
    for side in (1, 0):
        for k in range(1, 8):
            returns[side, k].wait_recv()
        combine(side, part, back, mixed)
        for k in (4, 3, 5, 2, 6, 1, 7):
            finals[side, k] = send(
                mixed.at[side, ORDER.index(k)], mixes.at[side, head], final_sems, 8 * side + k, head_peer(place, -k)
            )
            finals[side, k].start()
        mixes[side, head] = mixed[side, 0]
    for side in range(2):
        for k in range(1, 8):
            finals[side, k].wait_recv()
        for h in range(HEADS):
            whole[side, :, h * DIM : (h + 1) * DIM] = mixes[side, h]
    for load in loads[4:]:
        load.wait()
    for group in (legs, sends, gathers, returns, finals):
        for s in group.values():
            s.wait_send()


def project(mix, vproj, aproj, vout, aout):
    for side, weights, out in ((0, vproj, vout), (1, aproj, aout)):
        out[...] = jnp.dot(mix[side], weights[...], preferred_element_type=F32).astype(BF16)


def shards(vm, vv, am, av, vproj, aproj):
    vmem = pl.BlockSpec(memory_space=pltpu.VMEM)
    hbm = pl.BlockSpec(memory_space=pltpu.HBM)
    held = pl.pallas_call(
        kernel,
        out_shape=[pltpu.VMEM((2, ROWS, WIDTH), BF16)] + [pltpu.VMEM((WIDTH, WIDTH), BF16)] * 2,
        in_specs=[hbm] * 6,
        out_specs=[vmem] * 3,
        scratch_shapes=[
            pltpu.VMEM((4, ROWS, WIDTH), BF16),
            pltpu.VMEM((2, HEADS, 2, ROWS, DIM), BF16),
            pltpu.VMEM((2, 3, 2, ROWS, DIM), BF16),
            pltpu.VMEM((8, 2, 2, BLOCK, DIM), BF16),
            pltpu.VMEM((2, DIM + 16, TOKENS), BF16),
            pltpu.VMEM((TOKENS, BLOCK), F32),
            pltpu.VMEM((2, TOKENS, TOKENS), BF16),
            pltpu.VMEM((2, 8, STAT, DIM), BF16),
            pltpu.VMEM((2, 8, STAT, DIM), BF16),
            pltpu.VMEM((2, HEADS, ROWS, DIM), BF16),
            pltpu.VMEM((2, HEADS, ROWS, DIM), BF16),
            pltpu.SemaphoreType.DMA((2, 8)),
            pltpu.SemaphoreType.DMA((2, 16)),
            pltpu.SemaphoreType.DMA((2, 16 * len(PARTS))),
            pltpu.SemaphoreType.DMA((2, 16)),
            pltpu.SemaphoreType.DMA((2, 16)),
            pltpu.SemaphoreType.DMA((6,)),
        ],
        compiler_params=pltpu.CompilerParams(
            collective_id=0, has_side_effects=True, vmem_limit_bytes=KERNEL_VMEM
        ),
        name="attend",
    )(*(pltpu.with_memory_space_constraint(x, pltpu.HBM) for x in (vm, vv, am, av, vproj, aproj)))
    return pl.pallas_call(
        project,
        out_shape=[jax.ShapeDtypeStruct((ROWS, WIDTH), BF16)] * 2,
        in_specs=[vmem] * 3,
        out_specs=[vmem] * 2,
        compiler_params=pltpu.CompilerParams(vmem_limit_bytes=16 * 2**20),
        name="project",
    )(*(pltpu.with_memory_space_constraint(x, pltpu.VMEM) for x in held))


def solution(mesh):
    tokens = P(("vid", "aud"), None)
    return jax.shard_map(
        shards,
        mesh=mesh,
        in_specs=(tokens,) * 4 + (P(), P()),
        out_specs=(tokens, tokens),
        check_vma=False,
    )
```

```python
import math

import jax
import jax.numpy as jnp
from jax import lax
from jax.experimental import pallas as pl
from jax.experimental.pallas import tpu as pltpu
from jax.sharding import PartitionSpec as P

MESH = pl.DeviceIdType.MESH
HEADS = 8
DIM = 128
ROWS = 16
BLOCK = HEADS * ROWS
TOKENS = 8 * BLOCK
WIDTH = HEADS * DIM
STAT = BLOCK + 16
KERNEL_VMEM = 32 * 2**20
WIDE = 4
STEP = 2
ORDER = (0, 1, 7, 2, 6, 3, 5, 4)
PARTS = ((None, 0, 5), (0, 5, 8), (1, 5, 8))
SCALE = DIM ** (-0.5) * math.log2(math.e)
F32, BF16 = jnp.float32, jnp.bfloat16
NT = (((1,), (1,)), ((), ()))


def position():
    v, a = lax.axis_index("vid"), lax.axis_index("aud")
    return a % 4, v // 8, (a // 4) * 4 + (v // 2) % 4, v % 2


def device(place):
    x, y, z, c = place
    return ((y * 4 + z % 4) * 2 + c, (z // 4) * 4 + x)


def head_peer(place, k):
    x, y, z, c = place
    return x, y, (z + 2 * k + 16) % 16, c


def video_peer(place, k):
    x, y, z, c = place
    step = k // 2 if k >= 0 else -((-k) // 2)
    return (x + step + 4) % 4, y, z, (c + k) % 2 if k >= 0 else (c - k) % 2


def audio_peer(place, k):
    x, y, z, c = place
    step = k // 2 if k >= 0 else -((-k) // 2)
    return x, (y + step + 4) % 4, (z // 2) * 2 + (z + abs(k)) % 2, c


def send(src, dst, sems, n, place):
    return pltpu.make_async_remote_copy(
        src_ref=src,
        dst_ref=dst,
        send_sem=sems.at[0, n],
        recv_sem=sems.at[1, n],
        device_id=device(place),
        device_id_type=MESH,
    )


def weigh(tile, tops, probs):
    wide, step = WIDE * BLOCK, STEP * BLOCK

    def score(n, first):
        keys = tile[n : n + STEP, 0, 1].reshape(step, DIM)
        queries = tile[first : first + WIDE, 0, 0].reshape(wide, DIM)
        return lax.dot_general(keys, queries, NT, preferred_element_type=F32)

    peaks = [{}, {}]
    for first in range(0, 8, WIDE):
        peak = None
        for n in range(0, 8, STEP):
            tops_of = pl.ds(n * BLOCK, step)
            scores = score(n, first)
            top = scores.reshape(step // 8, 8, wide).max(0)
            peak = top if peak is None else jnp.maximum(peak, top)
            top = scores[:, :BLOCK]
            for s in range(1, WIDE):
                top = jnp.maximum(top, scores[:, s * BLOCK : (s + 1) * BLOCK])
            tops[tops_of] = jnp.maximum(tops[tops_of], top) if first else top
        peaks[0][first] = peak.max(0, keepdims=True).astype(BF16).astype(F32)
    for n in range(0, 8, STEP):
        rows = slice(n * BLOCK, n * BLOCK + step)
        across = tops[rows].max(1, keepdims=True).astype(BF16).astype(F32)
        for first in range(0, 8, WIDE):
            lanes = slice(first * BLOCK, first * BLOCK + wide)
            scores = score(n, first)
            probs[0, rows, lanes] = jnp.exp2((scores - peaks[0][first]) * SCALE).astype(BF16)
            probs[1, rows, lanes] = jnp.exp2((scores - across) * SCALE).astype(BF16)
    for first in range(0, 8, WIDE):
        peaks[1][first] = jnp.concatenate(
            [tops[n * BLOCK : (n + 1) * BLOCK].T.max(0, keepdims=True) for n in range(first, first + WIDE)], axis=1
        ).astype(BF16).astype(F32)
    return peaks


def gather_values(side, first, peak, values_t, probs, out):
    tokens = slice(first * BLOCK, (first + WIDE) * BLOCK)
    if side:
        num = lax.dot_general(values_t[1], probs[1, tokens], NT, preferred_element_type=F32)
    else:
        num = jnp.dot(values_t[0], probs[0, :, tokens], preferred_element_type=F32)
    total = num[DIM : DIM + 1]
    high = total.astype(BF16).astype(F32)
    row = lax.broadcasted_iota(jnp.int32, (16, WIDE * BLOCK), 0)
    stat = jnp.where(row == 0, peak, jnp.where(row == 1, high, jnp.where(row == 2, total - high, 0.0)))
    for s in range(WIDE):
        lanes = slice(s * BLOCK, (s + 1) * BLOCK)
        out[side, first + s, :BLOCK] = num[:DIM, lanes].astype(BF16)
        out[side, first + s, BLOCK:] = stat[:, lanes].astype(BF16)


def combine(side, part, back, mixed):
    def source(k):
        return part if k == 0 else back

    stats = [source(k)[side, k, BLOCK:].astype(F32) for k in range(8)]
    peaks = [s[0:1] for s in stats]
    top = peaks[0]
    for p in peaks[1:]:
        top = jnp.maximum(top, p)
    num = jnp.zeros((DIM, BLOCK), F32)
    total = jnp.zeros((1, BLOCK), F32)
    for k in range(8):
        gain = jnp.exp2((peaks[k] - top) * SCALE)
        total = total + gain * (stats[k][1:2] + stats[k][2:3])
        num = num + gain * source(k)[side, k, :BLOCK].astype(F32)
    mix = (num / total).T.astype(BF16)
    mixed[side] = mix.reshape(HEADS, ROWS, DIM)


def kernel(vm, vv, am, av, vproj, aproj, whole, vweights, aweights,
           tokens, staged, passing, tile, values_t, tops, probs, part, back, mixed, mixes,
           pass_sems, head_sems, gather_sems, return_sems, final_sems, local_sems):
    place = position()
    head = place[2] // 2
    barrier = pltpu.get_barrier_semaphore()
    greeted = [(head_peer, k) for k in (2, 6, 1, 7)] + [(peer, k) for peer in (video_peer, audio_peer) for k in range(1, 8)]
    for peer, k in greeted:
        pl.semaphore_signal(barrier, inc=1, device_id=device(peer(place, k)), device_id_type=MESH)
    loads = [
        pltpu.make_async_copy(array, tokens.at[n], local_sems.at[n]) for n, array in enumerate((vm, am, vv, av))
    ] + [
        pltpu.make_async_copy(vproj, vweights, local_sems.at[4]),
        pltpu.make_async_copy(aproj, aweights, local_sems.at[5]),
    ]
    for load in loads:
        load.start()

    for n in range(4):
        loads[n].wait()
        for h in range(HEADS):
            staged[n // 2, h, n % 2] = tokens[n, :, h * DIM : (h + 1) * DIM]
    for kind in range(2):
        tile[0, kind, :, :ROWS] = staged[kind, head]
    values_t[:, DIM:] = jnp.ones((2, 16, TOKENS), BF16)
    pl.semaphore_wait(barrier, len(greeted))

    def rows_of(k):
        return pl.ds(ORDER.index(k) * ROWS, ROWS)

    def columns(kind, k):
        return staged.at[kind, (head + k) % HEADS]

    legs, sends = {}, {}
    for kind in (0,):
        for n, (src, dst, via) in enumerate((
            (columns(kind, 4).at[0], passing.at[kind, 2, 0], 2),
            (columns(kind, 4).at[1], passing.at[kind, 2, 1], -2),
            (columns(kind, 3), passing.at[kind, 0], 2),
            (columns(kind, 5), passing.at[kind, 1], -2),
        )):
            legs[kind, n] = send(src, dst, pass_sems, 4 * kind + n, head_peer(place, via))
            legs[kind, n].start()
    for k in (1, 7, 2, 6):
        sends[k] = send(
            staged.at[:, (head + k) % HEADS], tile.at[0, :, :, rows_of(k)], head_sems, k, head_peer(place, k)
        )
        sends[k].start()
    for kind in (1,):
        for n, (src, dst, via) in enumerate((
            (columns(kind, 4).at[0], passing.at[kind, 2, 0], 2),
            (columns(kind, 4).at[1], passing.at[kind, 2, 1], -2),
            (columns(kind, 3), passing.at[kind, 0], 2),
            (columns(kind, 5), passing.at[kind, 1], -2),
        )):
            legs[kind, n] = send(src, dst, pass_sems, 4 * kind + n, head_peer(place, via))
            legs[kind, n].start()
    for kind in range(2):
        for n, (src, dst, to) in enumerate((
            (passing.at[kind, 2, 0], tile.at[0, kind, 0, rows_of(4)], 2),
            (passing.at[kind, 2, 1], tile.at[0, kind, 1, rows_of(4)], -2),
            (passing.at[kind, 0], tile.at[0, kind, :, rows_of(3)], 1),
            (passing.at[kind, 1], tile.at[0, kind, :, rows_of(5)], -1),
        )):
            legs[kind, n].wait_recv()
            sends[kind, n] = send(src, dst, head_sems, 8 + 4 * kind + n, head_peer(place, to))
            sends[kind, n].start()

    gathers = {}
    for n, (kind, first, last) in enumerate(PARTS):
        for key in (2, 6, 1, 7) if kind is None else ((kind, 0), (kind, 1), (kind, 2), (kind, 3)):
            sends[key].wait_recv()
        rows = pl.ds(first * ROWS, (last - first) * ROWS)
        kinds = slice(None) if kind is None else kind
        for k in (5, 4, 3, 7, 2, 6, 1):
            for side, peer in ((1, audio_peer), (0, video_peer)):
                sem = 16 * n + 8 * side + k
                gathers[n, side, k] = send(
                    tile.at[0, kinds, side, rows], tile.at[k, kinds, side, rows], gather_sems, sem, peer(place, k)
                )
                gathers[n, side, k].start()

    def arrive(kind):
        for n, side, k in gathers:
            if (PARTS[n][0] or 0) == kind:
                gathers[n, side, k].wait_recv()

    arrive(0)
    peaks = weigh(tile, tops, probs)
    arrive(1)
    for side in range(2):
        for k in range(8):
            values_t[side, :DIM, k * BLOCK : (k + 1) * BLOCK] = tile[k, 1, 1 - side].T
    returns = {}
    for first in range(8 - WIDE, -1, -WIDE):
        for side, peer in ((0, video_peer), (1, audio_peer)):
            gather_values(side, first, peaks[side][first], values_t, probs, part)
            for k in (first + 1, first, first + 3, first + 2):
                if k:
                    returns[side, k] = send(part.at[side, k], back.at[side, k], return_sems, 8 * side + k, peer(place, -k))
                    returns[side, k].start()

    finals = {}
    for side in (1, 0):
        for k in range(1, 8):
            returns[side, k].wait_recv()
        combine(side, part, back, mixed)
        for k in (4, 3, 5, 2, 6, 1, 7):
            finals[side, k] = send(
                mixed.at[side, ORDER.index(k)], mixes.at[side, head], final_sems, 8 * side + k, head_peer(place, -k)
            )
            finals[side, k].start()
        mixes[side, head] = mixed[side, 0]
    for side in range(2):
        for k in range(1, 8):
            finals[side, k].wait_recv()
        for h in range(HEADS):
            whole[side, :, h * DIM : (h + 1) * DIM] = mixes[side, h]
    for load in loads[4:]:
        load.wait()
    for group in (legs, sends, gathers, returns, finals):
        for s in group.values():
            s.wait_send()


def project(mix, vproj, aproj, vout, aout, held, sems):
    copies = []
    for side, weights, out in ((0, vproj, vout), (1, aproj, aout)):
        held[side] = jnp.dot(mix[side], weights[...], preferred_element_type=F32).astype(BF16)
        copies.append(pltpu.make_async_copy(held.at[side], out, sems.at[side]))
        copies[-1].start()
    for copy in copies:
        copy.wait()


def shards(vm, vv, am, av, vproj, aproj):
    vmem = pl.BlockSpec(memory_space=pltpu.VMEM)
    hbm = pl.BlockSpec(memory_space=pltpu.HBM)
    held = pl.pallas_call(
        kernel,
        out_shape=[pltpu.VMEM((2, ROWS, WIDTH), BF16)] + [pltpu.VMEM((WIDTH, WIDTH), BF16)] * 2,
        in_specs=[hbm] * 6,
        out_specs=[vmem] * 3,
        scratch_shapes=[
            pltpu.VMEM((4, ROWS, WIDTH), BF16),
            pltpu.VMEM((2, HEADS, 2, ROWS, DIM), BF16),
            pltpu.VMEM((2, 3, 2, ROWS, DIM), BF16),
            pltpu.VMEM((8, 2, 2, BLOCK, DIM), BF16),
            pltpu.VMEM((2, DIM + 16, TOKENS), BF16),
            pltpu.VMEM((TOKENS, BLOCK), F32),
            pltpu.VMEM((2, TOKENS, TOKENS), BF16),
            pltpu.VMEM((2, 8, STAT, DIM), BF16),
            pltpu.VMEM((2, 8, STAT, DIM), BF16),
            pltpu.VMEM((2, HEADS, ROWS, DIM), BF16),
            pltpu.VMEM((2, HEADS, ROWS, DIM), BF16),
            pltpu.SemaphoreType.DMA((2, 8)),
            pltpu.SemaphoreType.DMA((2, 16)),
            pltpu.SemaphoreType.DMA((2, 16 * len(PARTS))),
            pltpu.SemaphoreType.DMA((2, 16)),
            pltpu.SemaphoreType.DMA((2, 16)),
            pltpu.SemaphoreType.DMA((6,)),
        ],
        compiler_params=pltpu.CompilerParams(
            collective_id=0, has_side_effects=True, vmem_limit_bytes=KERNEL_VMEM
        ),
        name="attend",
    )(*(pltpu.with_memory_space_constraint(x, pltpu.HBM) for x in (vm, vv, am, av, vproj, aproj)))
    return pl.pallas_call(
        project,
        out_shape=[jax.ShapeDtypeStruct((ROWS, WIDTH), BF16)] * 2,
        in_specs=[vmem] * 3,
        out_specs=[pl.BlockSpec(memory_space=pl.ANY)] * 2,
        scratch_shapes=[pltpu.VMEM((2, ROWS, WIDTH), BF16), pltpu.SemaphoreType.DMA((2,))],
        compiler_params=pltpu.CompilerParams(vmem_limit_bytes=16 * 2**20),
        name="project",
    )(*(pltpu.with_memory_space_constraint(x, pltpu.VMEM) for x in held))


def solution(mesh):
    tokens = P(("vid", "aud"), None)
    return jax.shard_map(
        shards,
        mesh=mesh,
        in_specs=(tokens,) * 4 + (P(), P()),
        out_specs=(tokens, tokens),
        check_vma=False,
    )
```
